128 devices in a mesh: section: 8 (over x, core), row: 4 (over y), col: 4 (over z).
Axes of the slice: x: 4, y: 4, z: 4, core: 2. Of those that a mesh axis runs over, the one named last changes fastest.
Arguments:
- gate_grad: bfloat16 [16384, 5632], P('section', ('row', 'col')), parts along dimension 0, may hold values from -4 to 4
- up_grad: bfloat16 [16384, 5632], P('section', ('row', 'col')), parts along dimension 0, may hold values from -4 to 4
Outputs:
- gate_next: bfloat16 [16384, 5632], P('section', ('row', 'col')), parts along dimension 0
- up_next: bfloat16 [16384, 5632], P('section', ('row', 'col')), parts along dimension 0
The draws below stay inside these ranges and needn't reach their ends.
There are 8 independent parts, one for each index of `section`. The reference program is written for one: setup_inputs(seed, part) draws one part's arguments, and reference() takes and returns one part's arrays. A program takes and returns all parts, laid end to end along the dimension named above; each array names one. Nothing has to cross between parts.
All inputs are finite; a program needn't handle non-finite values.
Results may differ from the reference program's by a relative error of at most 0.022.
Values may be sent and summed in bfloat16 or wider, within the bound.
No kernel may reach another device: no remote copies, remote signals or barrier semaphores. Data moves between devices by JAX's collectives and lax.ppermute only.
A program may use at most 128 MiB of HBM per device.

```python
import jax
import jax.numpy as jnp
from jax import lax

COLS = 352
D = 2048
F = 5632
N_ROW = 4
N_COL = 4


def steps_of(own_key, dims, split, least, top_value):
    gain = 1.0
    for dim, shards_of in split:
        draws = jax.random.uniform(jax.random.fold_in(jax.random.fold_in(own_key, 6), dim), (shards_of,), jnp.float32, least / len(split), top_value / len(split))
        gain = gain * jnp.repeat(jnp.exp(draws), dims[dim] // shards_of).reshape((-1,) + (1,) * (len(dims) - 1 - dim))
    return gain


def normal_values(stream_key, extent, deviation, reach, shards=(), held_as=jnp.bfloat16):
    values = deviation * jax.random.normal(stream_key, extent, jnp.float32)
    if shards:
        values = values * steps_of(stream_key, extent, shards, -0.22, 0.18)
    return jnp.clip(values, -reach, reach).astype(held_as)


def setup_inputs(seed: int = 0, part: int = 0) -> dict:
    splits = jax.random.split(jax.random.key(seed), 3)
    part_splits = jax.random.split(jax.random.fold_in(splits[2], part), 3)
    gate_grad = normal_values(part_splits[0], (D, F), 0.65, 4.0, ((1, 16),))
    up_grad = normal_values(part_splits[1], (D, F), 0.65, 4.0, ((1, 16),))
    return dict(gate_grad=gate_grad, up_grad=up_grad)


COEF_A = 3.4445
COEF_B = -4.7750
COEF_C = 2.0315


def gram_of(iterate):
    groups = N_ROW * N_COL
    inverse_cols = 1.0 / F

    def add_group(running, group):
        columns_part = lax.dynamic_slice_in_dim(iterate, group * COLS, COLS, 1)
        partial_value = (jnp.dot(columns_part, columns_part.T, preferred_element_type=jnp.float32) * inverse_cols).astype(jnp.bfloat16)
        partial_value = lax.optimization_barrier(partial_value)
        return running + partial_value.astype(jnp.float32), None

    running, unused = lax.scan(add_group, jnp.zeros((D, D), jnp.float32), jnp.arange(groups, dtype=jnp.int32))
    return running


def newton_step(iterate):
    gram_full = gram_of(iterate)
    gram_low = gram_full.astype(jnp.bfloat16)
    squared = jnp.dot(gram_low, gram_low, preferred_element_type=jnp.float32)
    mixing = (COEF_B * gram_full + COEF_C * squared).astype(jnp.bfloat16)
    product = jnp.dot(mixing, iterate, preferred_element_type=jnp.float32)
    return (COEF_A * iterate.astype(jnp.float32) + product).astype(jnp.bfloat16)


def reference(gate_grad, up_grad):
    return (newton_step(gate_grad), newton_step(up_grad))
```

```python
import functools

import jax
import jax.numpy as jnp
from jax import lax
from jax.experimental import pallas as pl
from jax.experimental.pallas import tpu as pltpu
from jax.sharding import PartitionSpec as P

COEF_A = 3.4445
COEF_B = -4.775
COEF_C = 2.0315

AXES = ("section", "row", "col")
BLOCK = 128
VMEM_LIMIT = 56 * 1024 * 1024


def device_pairs(route):
    pairs = []
    for x in range(4):
        for core in range(2):
            for y in range(4):
                for z in range(4):
                    target = route(core, y, z)
                    if target is not None:
                        to_core, to_y, to_z = target
                        pairs.append(
                            (((x * 2 + core) * 4 + y) * 4 + z, ((x * 2 + to_core) * 4 + to_y) * 4 + to_z)
                        )
    return pairs


def outer(i):
    return i in (0, 3)


OTHER_CORE = device_pairs(lambda c, y, z: (1 - c, y, z))
GATE_OUT = device_pairs(lambda c, y, z: (0, y ^ 1, z) if c == (1 if outer(y) else 0) else None)
UP_OUT = device_pairs(lambda c, y, z: (1, y, z ^ 1) if c == (1 if outer(z) else 0) else None)
GATE_BACK = [(b, a) for a, b in GATE_OUT]
UP_BACK = [(b, a) for a, b in UP_OUT]
HOP_1 = device_pairs(lambda c, y, z: (c, y, z ^ 1) if c == 0 else (c, y ^ 1, z))
HOP_2 = device_pairs(lambda c, y, z: (c, y, 3 - z) if c == 0 else (c, 3 - y, z))
HOP_3 = device_pairs(lambda c, y, z: (c, 3 - y, z) if c == 0 else (c, y, 3 - z))


def send(values, pairs):
    return lax.ppermute(values, AXES, pairs)


def extend(wide, columns):
    rows = columns.shape[0]
    wide[0:rows, :] = columns[...]
    wide[rows : rows + rows // 2, :] = columns[0 : rows // 2, :]


def block_row(wide, index, span):
    first = pl.multiple_of(index * BLOCK, BLOCK)
    return lax.dot_general(
        wide[pl.ds(first, BLOCK), :],
        wide[pl.ds(first, span), :],
        (((1,), (1,)), ((), ())),
        preferred_element_type=jnp.float32,
    )


def first_terms_kernel(order, columns, terms, wide):
    extend(wide, columns)
    blocks, _, span = terms.shape

    def one(k, carry):
        terms[k] = block_row(wide, order[k], span)
        return carry

    lax.fori_loop(0, blocks, one, 0)


def first_terms(order, columns, span):
    rows, dev_cols = columns.shape
    return pl.pallas_call(
        first_terms_kernel,
        out_shape=jax.ShapeDtypeStruct((order.shape[0], BLOCK, span), jnp.float32),
        in_specs=[
            pl.BlockSpec(memory_space=pltpu.SMEM),
            pl.BlockSpec(memory_space=pltpu.VMEM),
        ],
        out_specs=pl.BlockSpec(memory_space=pltpu.VMEM),
        scratch_shapes=[pltpu.VMEM((rows + rows // 2, dev_cols), jnp.bfloat16)],
        compiler_params=pltpu.CompilerParams(vmem_limit_bytes=VMEM_LIMIT),
        cost_estimate=pl.CostEstimate(
            flops=2 * order.shape[0] * BLOCK * span * dev_cols, bytes_accessed=12000000, transcendentals=0
        ),
    )(order, columns)


def add_terms_kernel(first_block, scale, order, columns, terms, total, wide):
    extend(wide, columns)
    blocks, _, span = total.shape

    def one(k, carry):
        value = terms[first_block + k] + block_row(wide, order[first_block + k], span)
        total[k] = (value * scale).astype(total.dtype)
        return carry

    lax.fori_loop(0, blocks, one, 0)


def add_terms(order, columns, terms, first_block, blocks, scale, dtype):
    rows, dev_cols = columns.shape
    span = terms.shape[2]
    return pl.pallas_call(
        functools.partial(add_terms_kernel, first_block, scale),
        out_shape=jax.ShapeDtypeStruct((blocks, BLOCK, span), dtype),
        in_specs=[
            pl.BlockSpec(memory_space=pltpu.SMEM),
            pl.BlockSpec(memory_space=pltpu.VMEM),
            pl.BlockSpec(memory_space=pltpu.VMEM),
        ],
        out_specs=pl.BlockSpec(memory_space=pltpu.VMEM),
        scratch_shapes=[pltpu.VMEM((rows + rows // 2, dev_cols), jnp.bfloat16)],
        compiler_params=pltpu.CompilerParams(vmem_limit_bytes=VMEM_LIMIT),
        cost_estimate=pl.CostEstimate(
            flops=2 * blocks * BLOCK * span * dev_cols, bytes_accessed=12000000, transcendentals=0
        ),
    )(order, columns, terms)


def step_kernel(order, columns, *rest):
    pieces, (result, gram, low, linear) = rest[:-4], rest[-4:]
    rows = columns.shape[0]
    count = rows // BLOCK
    place = 0
    for piece in pieces:
        span = piece.shape[2]
        for k in range(piece.shape[0]):
            index = order[place]
            place += 1
            top = pl.multiple_of(index * BLOCK, BLOCK)
            for shift in range(span // BLOCK):
                left = pl.multiple_of(((index + shift) % count) * BLOCK, BLOCK)
                block = piece[k, :, shift * BLOCK : (shift + 1) * BLOCK]
                gram[pl.ds(top, BLOCK), pl.ds(left, BLOCK)] = block
                if 0 < shift < span // BLOCK - 1:
                    gram[pl.ds(left, BLOCK), pl.ds(top, BLOCK)] = block.T
    tile = 256

    def multiply(t, carry):
        at = pl.ds(pl.multiple_of(t * tile, tile), tile)
        value = jnp.dot(gram[at, :], columns[...], preferred_element_type=jnp.float32)
        low[at, :] = value.astype(jnp.bfloat16)
        linear[at, :] = COEF_A * columns[at, :].astype(jnp.float32) + COEF_B * value
        return carry

    lax.fori_loop(0, rows // tile, multiply, 0)

    def again(t, carry):
        at = pl.ds(pl.multiple_of(t * tile, tile), tile)
        value = jnp.dot(gram[at, :], low[...], preferred_element_type=jnp.float32)
        result[at, :] = (linear[at, :] + COEF_C * value).astype(jnp.bfloat16)
        return carry

    lax.fori_loop(0, rows // tile, again, 0)


def newton_step(order, columns, pieces):
    rows, dev_cols = columns.shape
    return pl.pallas_call(
        step_kernel,
        out_shape=jax.ShapeDtypeStruct(columns.shape, jnp.bfloat16),
        in_specs=[pl.BlockSpec(memory_space=pltpu.SMEM)]
        + [pl.BlockSpec(memory_space=pltpu.VMEM)] * (1 + len(pieces)),
        out_specs=pl.BlockSpec(memory_space=pltpu.VMEM),
        scratch_shapes=[
            pltpu.VMEM((rows, rows), jnp.bfloat16),
            pltpu.VMEM((rows, dev_cols), jnp.bfloat16),
            pltpu.VMEM((rows, dev_cols), jnp.float32),
        ],
        compiler_params=pltpu.CompilerParams(vmem_limit_bytes=VMEM_LIMIT),
        cost_estimate=pl.CostEstimate(
            flops=4 * rows * rows * dev_cols, bytes_accessed=8000000, transcendentals=0
        ),
    )(order, columns, *pieces)


def per_device(gate_grad, up_grad):
    rows, dev_cols = gate_grad.shape
    span = rows // 2 + BLOCK
    scale = 1.0 / (dev_cols * lax.axis_size(("row", "col")))
    core = lax.axis_index("section") % 2
    y = lax.axis_index("row")
    z = lax.axis_index("col")
    gate_first = (y == 0) | (y == 3)
    up_first = (z == 0) | (z == 3)
    on_gate = core == 0

    y_low, y_high = ((y == 1) | (y == 2)).astype(jnp.int32), (y >= 2).astype(jnp.int32)
    z_low, z_high = ((z == 1) | (z == 2)).astype(jnp.int32), (z >= 2).astype(jnp.int32)
    p = jnp.where(on_gate, z_low, y_low)
    q = jnp.where(on_gate, z_high, y_high)
    r = jnp.where(on_gate, y_high, z_high)

    def block_a(dp, dq, dr):
        return 4 * (p ^ dp) + 2 * (q ^ dq) + (r ^ dr)

    def block_b(dp, dq, dr):
        return 8 + 4 * (q ^ dq) + 2 * (p ^ dp) + (r ^ dr)

    order = jnp.stack(
        [
            block(dp, dq, dr)
            for dp, dq in ((1, 1), (1, 0), (0, 1), (0, 0))
            for block in (block_a, block_b)
            for dr in (0, 1)
        ]
    )

    from_gate = send(gate_grad, GATE_OUT)
    from_up = send(up_grad, UP_OUT)
    from_core = send(jnp.where(on_gate, up_grad, gate_grad), OTHER_CORE)
    own = jnp.where(
        on_gate,
        jnp.where(gate_first, gate_grad, from_core),
        jnp.where(up_first, from_core, up_grad),
    )
    terms = first_terms(order, own, span)
    partner = jnp.where(on_gate, from_gate, from_up)

    corner = add_terms(order, partner, terms, 0, 4, scale, jnp.bfloat16)
    got_a = send(corner[0:2], HOP_1)
    got_b = send(corner[2:4], HOP_2)
    rest = add_terms(order, partner, terms, 4, 12, scale, jnp.float32)
    side_1 = jnp.concatenate(
        [rest[0:2].astype(jnp.bfloat16), (rest[2:4] + got_b.astype(jnp.float32)).astype(jnp.bfloat16)]
    )
    side_2 = jnp.concatenate(
        [(rest[4:6] + got_a.astype(jnp.float32)).astype(jnp.bfloat16), rest[6:8].astype(jnp.bfloat16)]
    )
    got_1 = send(side_1, HOP_1)
    got_2 = send(side_2, HOP_2)
    mine = (
        (rest[8:12] + got_1.astype(jnp.float32) + got_2.astype(jnp.float32))
    ).reshape(2, 2, BLOCK, span)
    got_3 = send(mine[:, 1].astype(jnp.bfloat16), HOP_3)
    done = (mine[:, 0] + got_3.astype(jnp.float32)).astype(jnp.bfloat16)

    far = send(done, HOP_3)
    both = jnp.stack([done, far], axis=1).reshape(4, BLOCK, span)
    all_1 = send(both, HOP_1)
    all_2 = send(both, HOP_2)
    last_a = send(all_2[0:2], HOP_1)
    last_b = send(all_1[2:4], HOP_2)
    pieces = (last_a, last_b, all_1, all_2, both)

    partner_next = newton_step(order, partner, pieces)
    gate_back = send(partner_next, GATE_BACK)
    up_back = send(partner_next, UP_BACK)
    own_next = newton_step(order, own, pieces)
    core_back = send(own_next, OTHER_CORE)

    gate_kept = jnp.where(on_gate, own_next, core_back)
    up_kept = jnp.where(on_gate, core_back, own_next)
    gate_next = jnp.where(gate_first == on_gate, gate_kept, gate_back)
    up_next = jnp.where(up_first == on_gate, up_kept, up_back)
    return gate_next, up_next


def solution(mesh):
    placed = (P("section", ("row", "col")), P("section", ("row", "col")))
    return jax.shard_map(
        per_device,
        mesh=mesh,
        in_specs=placed,
        out_specs=placed,
        check_vma=False,
    )
```

```python
import functools

import jax
import jax.numpy as jnp
from jax import lax
from jax.experimental import pallas as pl
from jax.experimental.pallas import tpu as pltpu
from jax.sharding import PartitionSpec as P

COEF_A = 3.4445
COEF_B = -4.775
COEF_C = 2.0315

AXES = ("section", "row", "col")
BLOCK = 128
PAIR = 2 * BLOCK
TILE = 512
VMEM_LIMIT = 28 * 1024 * 1024
ANY = pl.BlockSpec(memory_space=pl.ANY)
SMEM = pl.BlockSpec(memory_space=pltpu.SMEM)
VMEM = pl.BlockSpec(memory_space=pltpu.VMEM)


def device_pairs(route):
    pairs = []
    for x in range(4):
        for core in range(2):
            for y in range(4):
                for z in range(4):
                    target = route(core, y, z)
                    if target is not None:
                        to_core, to_y, to_z = target
                        pairs.append(
                            (((x * 2 + core) * 4 + y) * 4 + z, ((x * 2 + to_core) * 4 + to_y) * 4 + to_z)
                        )
    return pairs


def outer(i):
    return i in (0, 3)


GATE_OUT = device_pairs(lambda c, y, z: (0, y ^ 1, z) if c == (1 if outer(y) else 0) else None)
UP_OUT = device_pairs(lambda c, y, z: (1, y, z ^ 1) if c == (1 if outer(z) else 0) else None)
GATE_OVER = device_pairs(lambda c, y, z: (0, y, z) if c == 1 and not outer(y) else None)
UP_OVER = device_pairs(lambda c, y, z: (1, y, z) if c == 0 and outer(z) else None)


def reverse(pairs):
    return [(b, a) for a, b in pairs]


HOP_1 = device_pairs(lambda c, y, z: (c, y, z ^ 1) if c == 0 else (c, y ^ 1, z))
HOP_2 = device_pairs(lambda c, y, z: (c, y, 3 - z) if c == 0 else (c, 3 - y, z))
HOP_3 = device_pairs(lambda c, y, z: (c, 3 - y, z) if c == 0 else (c, y, 3 - z))


def send(values, pairs):
    return lax.ppermute(values, AXES, pairs)


def params():
    return pltpu.CompilerParams(vmem_limit_bytes=VMEM_LIMIT)


def fetch_wide(choice, sources, wide, sems):
    rows = sources[0].shape[1]
    for k, source in enumerate(sources):

        @pl.when(choice == k)
        def _(source=source):
            whole = pltpu.make_async_copy(source, wide.at[:, 0:rows], sems.at[0])
            head = pltpu.make_async_copy(
                source.at[:, 0 : rows // 2], wide.at[:, rows : rows + rows // 2], sems.at[1]
            )
            whole.start()
            head.start()
            whole.wait()
            head.wait()


def block_pair(wide, index, span):
    first = pl.multiple_of(index * PAIR, PAIR)
    value = lax.dot_general(
        wide[:, pl.ds(first, PAIR)],
        wide[:, pl.ds(first, span + BLOCK)],
        (((0,), (0,)), ((), ())),
        preferred_element_type=jnp.float32,
    )
    return value[0:BLOCK, 0:span], value[BLOCK:PAIR, BLOCK : span + BLOCK]


def own_terms_kernel(scale, order, choice, *rest):
    sources, (corner, others, wide, sems) = rest[:-4], rest[-4:]
    fetch_wide(choice[0], sources, wide, sems)
    span = corner.shape[2]
    for out, start, pairs in ((corner, 0, 2), (others, 2, 6)):

        def one(g, carry, out=out, start=start):
            upper, lower = block_pair(wide, order[start + g], span)
            out[2 * g] = (upper * scale).astype(out.dtype)
            out[2 * g + 1] = (lower * scale).astype(out.dtype)
            return carry

        lax.fori_loop(0, pairs, one, 0)


def own_terms(order, choice, sources, scale):
    dev_cols, rows = sources[0].shape
    span = rows // 2 + BLOCK
    return pl.pallas_call(
        functools.partial(own_terms_kernel, scale),
        out_shape=[jax.ShapeDtypeStruct((n, BLOCK, span), jnp.bfloat16) for n in (4, 12)],
        in_specs=[SMEM, SMEM] + [ANY] * len(sources),
        out_specs=[VMEM, VMEM],
        scratch_shapes=[
            pltpu.VMEM((dev_cols, rows + rows // 2), jnp.bfloat16),
            pltpu.SemaphoreType.DMA((2,)),
        ],
        compiler_params=params(),
        cost_estimate=pl.CostEstimate(
            flops=2 * rows * span * dev_cols, bytes_accessed=20000000, transcendentals=0
        ),
    )(order, choice, *sources)


def add_terms_kernel(scale, start, order, choice, *rest):
    sources, terms, outs, (wide, sems) = rest[:2], rest[2], rest[3:-2], rest[-2:]
    fetch_wide(choice[1], sources, wide, sems)
    span = terms.shape[2]
    done = 0
    for out in outs:

        def one(g, carry, out=out, done=done):
            upper, lower = block_pair(wide, order[start + done + g], span)
            at = 2 * (done + g)
            out[2 * g] = (upper * scale + terms[at].astype(jnp.float32)).astype(out.dtype)
            out[2 * g + 1] = (lower * scale + terms[at + 1].astype(jnp.float32)).astype(out.dtype)
            return carry

        lax.fori_loop(0, out.shape[0] // 2, one, 0)
        done += out.shape[0] // 2


def add_terms(order, choice, sources, terms, start, counts, scale):
    dev_cols, rows = sources[0].shape
    span = rows // 2 + BLOCK
    return pl.pallas_call(
        functools.partial(add_terms_kernel, scale, start),
        out_shape=[jax.ShapeDtypeStruct((n, BLOCK, span), jnp.bfloat16) for n in counts],
        in_specs=[SMEM, SMEM] + [ANY] * len(sources) + [VMEM],
        out_specs=[VMEM] * len(counts),
        scratch_shapes=[
            pltpu.VMEM((dev_cols, rows + rows // 2), jnp.bfloat16),
            pltpu.SemaphoreType.DMA((2,)),
        ],
        compiler_params=params(),
        cost_estimate=pl.CostEstimate(
            flops=2 * sum(counts) * BLOCK * span * dev_cols, bytes_accessed=10000000, transcendentals=0
        ),
    )(order, choice, *sources, terms)


def unpack_kernel(start, order, *rest):
    pieces, gram = rest[:-1], rest[-1]
    count = gram.shape[0] // BLOCK
    place = start
    for piece in pieces:
        span = piece.shape[2]
        for k in range(piece.shape[0]):
            index = 2 * order[place // 2] + place % 2
            place += 1
            top = pl.multiple_of(index * BLOCK, BLOCK)
            for shift in range(span // BLOCK):
                left = pl.multiple_of(((index + shift) % count) * BLOCK, BLOCK)
                block = piece[k, :, shift * BLOCK : (shift + 1) * BLOCK]
                gram[pl.ds(top, BLOCK), pl.ds(left, BLOCK)] = block
                if 0 < shift < span // BLOCK - 1:
                    gram[pl.ds(left, BLOCK), pl.ds(top, BLOCK)] = block.T


def unpack(order, pieces, start, rows):
    return pl.pallas_call(
        functools.partial(unpack_kernel, start),
        out_shape=jax.ShapeDtypeStruct((rows, rows), jnp.bfloat16),
        in_specs=[SMEM] + [VMEM] * len(pieces),
        out_specs=VMEM,
        compiler_params=params(),
        cost_estimate=pl.CostEstimate(flops=0, bytes_accessed=20000000, transcendentals=0),
    )(order, *pieces)


def step_kernel(which, order, choice, *rest):
    sources, (gram_in, last_a, last_b, result, gram, columns, low, linear, sems) = rest[:-9], rest[-9:]
    rows = gram.shape[0]
    load = pltpu.make_async_copy(gram_in, gram, sems.at[0])
    load.start()
    for k, source in enumerate(sources):

        @pl.when(choice[which] == k)
        def _(source=source):
            fetch = pltpu.make_async_copy(source, columns, sems.at[1])
            fetch.start()
            fetch.wait()

    load.wait()
    unpack_kernel(0, order, last_a, last_b, gram)

    def multiply(t, carry):
        at = pl.ds(pl.multiple_of(t * TILE, TILE), TILE)
        value = jnp.dot(columns[...], gram[:, at], preferred_element_type=jnp.float32)
        low[:, at] = value.astype(jnp.bfloat16)
        linear[:, at] = COEF_A * columns[:, at].astype(jnp.float32) + COEF_B * value
        return carry

    lax.fori_loop(0, rows // TILE, multiply, 0)

    def again(t, carry):
        at = pl.ds(pl.multiple_of(t * TILE, TILE), TILE)
        value = jnp.dot(low[...], gram[:, at], preferred_element_type=jnp.float32)
        result[:, at] = (linear[:, at] + COEF_C * value).astype(jnp.bfloat16)
        return carry

    lax.fori_loop(0, rows // TILE, again, 0)


def newton_step(which, order, choice, sources, gram, last_a, last_b):
    dev_cols, rows = sources[0].shape
    return pl.pallas_call(
        functools.partial(step_kernel, which),
        out_shape=jax.ShapeDtypeStruct((dev_cols, rows), jnp.bfloat16),
        in_specs=[SMEM, SMEM] + [ANY] * (len(sources) + 1) + [VMEM, VMEM],
        out_specs=VMEM,
        scratch_shapes=[
            pltpu.VMEM((rows, rows), jnp.bfloat16),
            pltpu.VMEM((dev_cols, rows), jnp.bfloat16),
            pltpu.VMEM((dev_cols, rows), jnp.bfloat16),
            pltpu.VMEM((dev_cols, rows), jnp.float32),
            pltpu.SemaphoreType.DMA((2,)),
        ],
        compiler_params=params(),
        cost_estimate=pl.CostEstimate(
            flops=4 * rows * rows * dev_cols, bytes_accessed=12000000, transcendentals=0
        ),
    )(order, choice, *sources, gram, last_a, last_b)


def add(*terms):
    return sum(t.astype(jnp.float32) for t in terms).astype(jnp.bfloat16)


def per_device(gate_grad, up_grad):
    rows, dev_cols = gate_grad.shape
    scale = 1.0 / (dev_cols * lax.axis_size(("row", "col")))
    gate, up = gate_grad.T, up_grad.T
    on_up = lax.axis_index("section") % 2
    y = lax.axis_index("row")
    z = lax.axis_index("col")
    y_low, y_high = ((y == 1) | (y == 2)).astype(jnp.int32), (y >= 2).astype(jnp.int32)
    z_low, z_high = ((z == 1) | (z == 2)).astype(jnp.int32), (z >= 2).astype(jnp.int32)
    on_gate = on_up == 0
    p = jnp.where(on_gate, z_low, y_low)
    q = jnp.where(on_gate, z_high, y_high)
    gate_part, up_part = y_low, z_low
    order = jnp.stack(
        [
            4 * stream + 2 * (p ^ dp) + (q ^ dq)
            for dp, dq in ((1, 1), (1, 0), (0, 1), (0, 0))
            for stream in (0, 1)
        ]
    )
    own_choice = jnp.where(on_gate, 2 * gate_part, 1 + 2 * (1 - up_part))
    choice = jnp.stack([own_choice, on_up])

    gate_over = send(gate, GATE_OVER)
    up_over = send(up, UP_OVER)
    gate_in = send(gate, GATE_OUT)
    up_in = send(up, UP_OUT)
    own = (gate, up, gate_over, up_over)
    partner = (gate_in, up_in)
    corner_terms, other_terms = own_terms(order, choice, own, scale)

    (corner,) = add_terms(order, choice, partner, corner_terms, 0, (4,), scale)
    got_a = send(corner[0:2], HOP_1)
    got_b = send(corner[2:4], HOP_2)
    side_1, side_2, mine = add_terms(order, choice, partner, other_terms, 2, (4, 4, 4), scale)
    got_1 = send(side_1.at[2:4].set(add(side_1[2:4], got_b)), HOP_1)
    got_2 = send(side_2.at[0:2].set(add(side_2[0:2], got_a)), HOP_2)
    mine = add(mine, got_1, got_2)
    total = add(mine, send(mine, HOP_3))

    all_1 = send(total, HOP_1)
    all_2 = send(total, HOP_2)
    last_a = send(all_2[0:2], HOP_1)
    last_b = send(all_1[2:4], HOP_2)
    gram = unpack(order, (all_1, all_2, total), 4, rows)

    partner_next = newton_step(1, order, choice, partner, gram, last_a, last_b)
    gate_back = send(partner_next, reverse(GATE_OUT))
    up_back = send(partner_next, reverse(UP_OUT))
    last_a, partner_next = lax.optimization_barrier((last_a, partner_next))
    own_next = newton_step(0, order, choice, own, gram, last_a, last_b)
    over_back = send(own_next, reverse(GATE_OVER) + reverse(UP_OVER))

    gate_next = jnp.where(gate_part == on_up, own_next, gate_back)
    up_next = jnp.where(up_part == on_up, own_next, up_back)
    gate_next, up_next = lax.optimization_barrier((gate_next, up_next))
    gate_next = jnp.where((gate_part == on_up) & (on_up == 1), over_back, gate_next)
    up_next = jnp.where((up_part == on_up) & on_gate, over_back, up_next)
    return gate_next.T, up_next.T


def solution(mesh):
    placed = (P("section", ("row", "col")), P("section", ("row", "col")))
    return jax.shard_map(
        per_device,
        mesh=mesh,
        in_specs=placed,
        out_specs=placed,
        check_vma=False,
    )
```

```python
import functools

import jax
import jax.numpy as jnp
from jax import lax
from jax.experimental import pallas as pl
from jax.experimental.pallas import tpu as pltpu
from jax.sharding import PartitionSpec as P

COEF_A = 3.4445
COEF_B = -4.775
COEF_C = 2.0315

AXES = ("section", "row", "col")
BLOCK = 128
PAIR = 2 * BLOCK
TILE = 512
VMEM_LIMIT = 28 * 1024 * 1024
ANY = pl.BlockSpec(memory_space=pl.ANY)
SMEM = pl.BlockSpec(memory_space=pltpu.SMEM)
VMEM = pl.BlockSpec(memory_space=pltpu.VMEM)


def device_pairs(route):
    pairs = []
    for x in range(4):
        for core in range(2):
            for y in range(4):
                for z in range(4):
                    target = route(core, y, z)
                    if target is not None:
                        to_core, to_y, to_z = target
                        pairs.append(
                            (((x * 2 + core) * 4 + y) * 4 + z, ((x * 2 + to_core) * 4 + to_y) * 4 + to_z)
                        )
    return pairs


def outer(i):
    return i in (0, 3)


GATE_OUT = device_pairs(lambda c, y, z: (0, y ^ 1, z) if c == (1 if outer(y) else 0) else None)
UP_OUT = device_pairs(lambda c, y, z: (1, y, z ^ 1) if c == (1 if outer(z) else 0) else None)
OVER = device_pairs(lambda c, y, z: (1 - c, y, z) if (outer(z) if c == 0 else not outer(y)) else None)


def reverse(pairs):
    return [(b, a) for a, b in pairs]


HOP_1 = device_pairs(lambda c, y, z: (c, y, z ^ 1) if c == 0 else (c, y ^ 1, z))
HOP_2 = device_pairs(lambda c, y, z: (c, y, 3 - z) if c == 0 else (c, 3 - y, z))
HOP_3 = device_pairs(lambda c, y, z: (c, 3 - y, z) if c == 0 else (c, y, 3 - z))


def send(values, pairs):
    return lax.ppermute(values, AXES, pairs)


def params():
    return pltpu.CompilerParams(vmem_limit_bytes=VMEM_LIMIT)


def fetch_wide(choice, sources, wide, sems):
    rows = sources[0].shape[1]
    for k, source in enumerate(sources):

        @pl.when(choice == k)
        def _(source=source):
            whole = pltpu.make_async_copy(source, wide.at[:, 0:rows], sems.at[0])
            head = pltpu.make_async_copy(
                source.at[:, 0 : rows // 2], wide.at[:, rows : rows + rows // 2], sems.at[1]
            )
            whole.start()
            head.start()
            whole.wait()
            head.wait()


def block_pair(wide, index, span):
    first = pl.multiple_of(index * PAIR, PAIR)
    value = lax.dot_general(
        wide[:, pl.ds(first, PAIR)],
        wide[:, pl.ds(first, span + BLOCK)],
        (((0,), (0,)), ((), ())),
        preferred_element_type=jnp.float32,
    )
    return value[0:BLOCK, 0:span], value[BLOCK:PAIR, BLOCK : span + BLOCK]


def own_terms_kernel(scale, order, choice, *rest):
    sources, (corner, others, wide, sems) = rest[:-4], rest[-4:]
    fetch_wide(choice[0], sources, wide, sems)
    span = corner.shape[2]
    for out, start, pairs in ((corner, 0, 2), (others, 2, 6)):

        def one(g, carry, out=out, start=start):
            upper, lower = block_pair(wide, order[start + g], span)
            out[2 * g] = (upper * scale).astype(out.dtype)
            out[2 * g + 1] = (lower * scale).astype(out.dtype)
            return carry

        lax.fori_loop(0, pairs, one, 0)


def own_terms(order, choice, sources, scale):
    dev_cols, rows = sources[0].shape
    span = rows // 2 + BLOCK
    return pl.pallas_call(
        functools.partial(own_terms_kernel, scale),
        out_shape=[jax.ShapeDtypeStruct((n, BLOCK, span), jnp.bfloat16) for n in (4, 12)],
        in_specs=[SMEM, SMEM] + [ANY] * len(sources),
        out_specs=[VMEM, VMEM],
        scratch_shapes=[
            pltpu.VMEM((dev_cols, rows + rows // 2), jnp.bfloat16),
            pltpu.SemaphoreType.DMA((2,)),
        ],
        compiler_params=params(),
        cost_estimate=pl.CostEstimate(
            flops=2 * rows * span * dev_cols, bytes_accessed=20000000, transcendentals=0
        ),
    )(order, choice, *sources)


def add_terms_kernel(scale, start, order, choice, *rest):
    sources, terms, outs, (wide, sems) = rest[:2], rest[2], rest[3:-2], rest[-2:]
    fetch_wide(choice[1], sources, wide, sems)
    span = terms.shape[2]
    done = 0
    for upper_out, lower_out in zip(outs[0::2], outs[1::2]):
        for g in range(upper_out.shape[0]):
            upper, lower = block_pair(wide, order[start + done], span)
            at = 2 * done
            upper_out[g] = (upper * scale + terms[at].astype(jnp.float32)).astype(upper_out.dtype)
            lower_out[g] = (lower * scale + terms[at + 1].astype(jnp.float32)).astype(lower_out.dtype)
            done += 1


def add_terms(order, choice, sources, terms, start, counts, scale):
    dev_cols, rows = sources[0].shape
    span = rows // 2 + BLOCK
    shapes = [n for n in counts for half in (0, 1)]
    return pl.pallas_call(
        functools.partial(add_terms_kernel, scale, start),
        out_shape=[jax.ShapeDtypeStruct((n, BLOCK, span), jnp.bfloat16) for n in shapes],
        in_specs=[SMEM, SMEM] + [ANY] * len(sources) + [VMEM],
        out_specs=[VMEM] * len(shapes),
        scratch_shapes=[
            pltpu.VMEM((dev_cols, rows + rows // 2), jnp.bfloat16),
            pltpu.SemaphoreType.DMA((2,)),
        ],
        compiler_params=params(),
        cost_estimate=pl.CostEstimate(
            flops=4 * sum(counts) * BLOCK * span * dev_cols, bytes_accessed=10000000, transcendentals=0
        ),
    )(order, choice, *sources, terms)


def place_blocks(places, order, pieces, gram):
    count = gram.shape[0] // BLOCK
    for (place, half), piece in zip(places, pieces):
        span = piece.shape[2]
        for k in range(piece.shape[0]):
            index = 2 * order[place + k] + half
            top = pl.multiple_of(index * BLOCK, BLOCK)
            for shift in range(span // BLOCK):
                left = pl.multiple_of(((index + shift) % count) * BLOCK, BLOCK)
                block = piece[k, :, shift * BLOCK : (shift + 1) * BLOCK]
                gram[pl.ds(top, BLOCK), pl.ds(left, BLOCK)] = block
                if 0 < shift < span // BLOCK - 1:
                    gram[pl.ds(left, BLOCK), pl.ds(top, BLOCK)] = block.T


def unpack_kernel(places, order, *rest):
    place_blocks(places, order, rest[:-1], rest[-1])


def unpack(order, pieces, places, rows):
    return pl.pallas_call(
        functools.partial(unpack_kernel, places),
        out_shape=jax.ShapeDtypeStruct((rows, rows), jnp.bfloat16),
        in_specs=[SMEM] + [VMEM] * len(pieces),
        out_specs=VMEM,
        compiler_params=params(),
        cost_estimate=pl.CostEstimate(flops=0, bytes_accessed=20000000, transcendentals=0),
    )(order, *pieces)


LAST_PLACES = ((0, 0), (1, 0), (0, 1), (1, 1))


def step_kernel(which, order, choice, *rest):
    sources, lasts = rest[:-11], rest[-10:-6]
    gram_in, (result, gram, columns, low, linear, sems) = rest[-11], rest[-6:]
    rows = gram.shape[0]
    load = pltpu.make_async_copy(gram_in, gram, sems.at[0])
    load.start()
    for k, source in enumerate(sources):

        @pl.when(choice[which] == k)
        def _(source=source):
            fetch = pltpu.make_async_copy(source, columns, sems.at[1])
            fetch.start()
            fetch.wait()

    load.wait()
    place_blocks(LAST_PLACES, order, lasts, gram)

    def multiply(t, carry):
        at = pl.ds(pl.multiple_of(t * TILE, TILE), TILE)
        value = jnp.dot(columns[...], gram[:, at], preferred_element_type=jnp.float32)
        low[:, at] = value.astype(jnp.bfloat16)
        linear[:, at] = COEF_A * columns[:, at].astype(jnp.float32) + COEF_B * value
        return carry

    lax.fori_loop(0, rows // TILE, multiply, 0)

    def again(t, carry):
        at = pl.ds(pl.multiple_of(t * TILE, TILE), TILE)
        value = jnp.dot(low[...], gram[:, at], preferred_element_type=jnp.float32)
        result[:, at] = (linear[:, at] + COEF_C * value).astype(jnp.bfloat16)
        return carry

    lax.fori_loop(0, rows // TILE, again, 0)


def newton_step(which, order, choice, sources, gram, lasts):
    dev_cols, rows = sources[0].shape
    return pl.pallas_call(
        functools.partial(step_kernel, which),
        out_shape=jax.ShapeDtypeStruct((dev_cols, rows), jnp.bfloat16),
        in_specs=[SMEM, SMEM] + [ANY] * (len(sources) + 1) + [VMEM] * len(lasts),
        out_specs=VMEM,
        scratch_shapes=[
            pltpu.VMEM((rows, rows), jnp.bfloat16),
            pltpu.VMEM((dev_cols, rows), jnp.bfloat16),
            pltpu.VMEM((dev_cols, rows), jnp.bfloat16),
            pltpu.VMEM((dev_cols, rows), jnp.float32),
            pltpu.SemaphoreType.DMA((2,)),
        ],
        compiler_params=params(),
        cost_estimate=pl.CostEstimate(
            flops=4 * rows * rows * dev_cols, bytes_accessed=12000000, transcendentals=0
        ),
    )(order, choice, *sources, gram, *lasts)


def token_kernel(gate_back, up_back, token):
    token[...] = jnp.zeros_like(token)


def after(*arrays):
    return pl.pallas_call(
        token_kernel,
        out_shape=jax.ShapeDtypeStruct((8, BLOCK), jnp.float32),
        in_specs=[ANY] * len(arrays),
        out_specs=VMEM,
    )(*arrays)


def finish_kernel(pick, token, own, over, gate_back, up_back, gate_out, up_out, sems):
    copies = [
        (pick[n] == k, pltpu.make_async_copy(source, out, sems.at[n]))
        for n, (back, out) in enumerate(((gate_back, gate_out), (up_back, up_out)))
        for k, source in enumerate((own, over, back))
    ]
    for wanted, copy in copies:
        pl.when(wanted)(copy.start)
    for wanted, copy in copies:
        pl.when(wanted)(copy.wait)


def finish(pick, own, over, gate_back, up_back):
    shape = jax.ShapeDtypeStruct(own.shape, own.dtype)
    return pl.pallas_call(
        finish_kernel,
        out_shape=[shape, shape],
        in_specs=[SMEM] + [ANY] * 5,
        out_specs=[VMEM, VMEM],
        scratch_shapes=[pltpu.SemaphoreType.DMA((2,))],
    )(pick, after(gate_back, up_back), own, over, gate_back, up_back)


def add(*terms):
    return sum(t.astype(jnp.float32) for t in terms).astype(jnp.bfloat16)


def per_device(gate_grad, up_grad):
    rows, dev_cols = gate_grad.shape
    scale = 1.0 / (dev_cols * lax.axis_size(("row", "col")))
    gate, up = gate_grad.T, up_grad.T
    on_up = lax.axis_index("section") % 2
    y = lax.axis_index("row")
    z = lax.axis_index("col")
    y_low, y_high = ((y == 1) | (y == 2)).astype(jnp.int32), (y >= 2).astype(jnp.int32)
    z_low, z_high = ((z == 1) | (z == 2)).astype(jnp.int32), (z >= 2).astype(jnp.int32)
    on_gate = on_up == 0
    p = jnp.where(on_gate, z_low, y_low)
    q = jnp.where(on_gate, z_high, y_high)
    gate_part, up_part = y_low, z_low
    order = jnp.stack(
        [
            4 * stream + 2 * (p ^ dp) + (q ^ dq)
            for dp, dq in ((1, 1), (1, 0), (0, 1), (0, 0))
            for stream in (0, 1)
        ]
    )
    own_choice = jnp.where(on_gate, 2 * gate_part, 2 - up_part)
    choice = jnp.stack([own_choice, on_up])

    gate_in = send(gate, GATE_OUT)
    up_in = send(up, UP_OUT)
    over = send(jnp.where(on_gate, up, gate), OVER)
    own = (gate, up, over)
    partner = (gate_in, up_in)
    corner_terms, other_terms = own_terms(order, choice, own, scale)

    corner = add_terms(order, choice, partner, corner_terms, 0, (1, 1), scale)
    got_a = [send(corner[half], HOP_1) for half in (0, 1)]
    got_b = [send(corner[2 + half], HOP_2) for half in (0, 1)]
    rest = add_terms(order, choice, partner, other_terms, 2, (2, 2, 2), scale)
    totals, ones, twos, lasts, places = [], [], [], [], []
    for half in (0, 1):
        side_1, side_2, mine = rest[half], rest[2 + half], rest[4 + half]
        got_1 = send(side_1.at[1:2].set(add(side_1[1:2], got_b[half])), HOP_1)
        got_2 = send(side_2.at[0:1].set(add(side_2[0:1], got_a[half])), HOP_2)
        mine = add(mine, got_1, got_2)
        totals.append(add(mine, send(mine, HOP_3)))

    for half in (0, 1):
        ones.append(send(totals[half], HOP_1))
        twos.append(send(totals[half], HOP_2))
    for half in (0, 1):
        lasts.append(send(twos[half][0:1], HOP_1))
        lasts.append(send(ones[half][1:2], HOP_2))
    gram = unpack(
        order,
        ones + twos + totals,
        ((2, 0), (2, 1), (4, 0), (4, 1), (6, 0), (6, 1)),
        rows,
    )

    partner_next = newton_step(1, order, choice, partner, gram, lasts)
    gate_back = send(partner_next, reverse(GATE_OUT))
    up_back = send(partner_next, reverse(UP_OUT))
    lasts[0], partner_next = lax.optimization_barrier((lasts[0], partner_next))
    own_next = newton_step(0, order, choice, own, gram, lasts)
    over_back = send(own_next, reverse(OVER))

    pick = jnp.stack(
        [
            jnp.where(gate_part == on_up, on_up, 2),
            jnp.where(up_part == on_up, 1 - on_up, 2),
        ]
    )
    gate_next, up_next = finish(pick, own_next, over_back, gate_back, up_back)
    return gate_next.T, up_next.T


def solution(mesh):
    placed = (P("section", ("row", "col")), P("section", ("row", "col")))
    return jax.shard_map(
        per_device,
        mesh=mesh,
        in_specs=placed,
        out_specs=placed,
        check_vma=False,
    )
```

```python
import functools

import jax
import jax.numpy as jnp
from jax import lax
from jax.experimental import pallas as pl
from jax.experimental.pallas import tpu as pltpu
from jax.sharding import PartitionSpec as P

COEF_A = 3.4445
COEF_B = -4.775
COEF_C = 2.0315

AXES = ("section", "row", "col")
BLOCK = 128
PAIR = 2 * BLOCK
TILE = 1024
OUT_TILES = ((0, 1024), (1024, 512), (1536, 512))
VMEM_LIMIT = 28 * 1024 * 1024
ANY = pl.BlockSpec(memory_space=pl.ANY)
SMEM = pl.BlockSpec(memory_space=pltpu.SMEM)
VMEM = pl.BlockSpec(memory_space=pltpu.VMEM)


def device_pairs(route):
    pairs = []
    for x in range(4):
        for core in range(2):
            for y in range(4):
                for z in range(4):
                    target = route(core, y, z)
                    if target is not None:
                        to_core, to_y, to_z = target
                        pairs.append(
                            (((x * 2 + core) * 4 + y) * 4 + z, ((x * 2 + to_core) * 4 + to_y) * 4 + to_z)
                        )
    return pairs


def outer(i):
    return i in (0, 3)


GATE_OUT = device_pairs(lambda c, y, z: (0, y ^ 1, z) if c == (1 if outer(y) else 0) else None)
UP_OUT = device_pairs(lambda c, y, z: (1, y, z ^ 1) if c == (1 if outer(z) else 0) else None)
OVER = device_pairs(lambda c, y, z: (1 - c, y, z) if (outer(z) if c == 0 else not outer(y)) else None)


def reverse(pairs):
    return [(b, a) for a, b in pairs]


HOP_1 = device_pairs(lambda c, y, z: (c, y, z ^ 1) if c == 0 else (c, y ^ 1, z))
HOP_2 = device_pairs(lambda c, y, z: (c, y, 3 - z) if c == 0 else (c, 3 - y, z))
HOP_3 = device_pairs(lambda c, y, z: (c, 3 - y, z) if c == 0 else (c, y, 3 - z))


def send(values, pairs):
    return lax.ppermute(values, AXES, pairs)


def params():
    return pltpu.CompilerParams(vmem_limit_bytes=VMEM_LIMIT)


def fetches(chosen, sources, columns, sems):
    copies = []
    for k, parts in enumerate((sources[0:1], sources[1:2], sources[2:])):
        first = 0
        for n, part in enumerate(parts):
            at = slice(first, first + part.shape[0])
            first += part.shape[0]
            copies.append((chosen == k, pltpu.make_async_copy(part, columns.at[at, :], sems.at[n])))
    for wanted, copy in copies:
        pl.when(wanted)(copy.start)
    return copies


def finish_fetches(copies):
    for wanted, copy in copies:
        pl.when(wanted)(copy.wait)


def fetch_wide(chosen, sources, wide, sems):
    rows = sources[0].shape[1]
    finish_fetches(fetches(chosen, sources, wide.at[:, 0:rows], sems))
    wide[:, rows : rows + rows // 2] = wide[:, 0 : rows // 2]


def block_pair(wide, index, span):
    first = pl.multiple_of(index * PAIR, PAIR)
    value = lax.dot_general(
        wide[:, pl.ds(first, PAIR)],
        wide[:, pl.ds(first, span + BLOCK)],
        (((0,), (0,)), ((), ())),
        preferred_element_type=jnp.float32,
    )
    return value[0:BLOCK, 0:span], value[BLOCK:PAIR, BLOCK : span + BLOCK]


def own_terms_kernel(scale, order, choice, *rest):
    sources, (corner, others, wide, sems) = rest[:-4], rest[-4:]
    fetch_wide(choice[0], sources, wide, sems)
    span = corner.shape[2]
    for out, start, pairs in ((corner, 0, 2), (others, 2, 6)):

        def one(g, carry, out=out, start=start):
            upper, lower = block_pair(wide, order[start + g], span)
            out[2 * g] = (upper * scale).astype(out.dtype)
            out[2 * g + 1] = (lower * scale).astype(out.dtype)
            return carry

        lax.fori_loop(0, pairs, one, 0)


def own_terms(order, choice, sources, scale):
    dev_cols, rows = sources[0].shape
    span = rows // 2 + BLOCK
    return pl.pallas_call(
        functools.partial(own_terms_kernel, scale),
        out_shape=[jax.ShapeDtypeStruct((n, BLOCK, span), jnp.bfloat16) for n in (4, 12)],
        in_specs=[SMEM, SMEM] + [ANY] * len(sources),
        out_specs=[VMEM, VMEM],
        scratch_shapes=[
            pltpu.VMEM((dev_cols, rows + rows // 2), jnp.bfloat16),
            pltpu.SemaphoreType.DMA((2,)),
        ],
        compiler_params=params(),
        cost_estimate=pl.CostEstimate(
            flops=2 * rows * span * dev_cols, bytes_accessed=20000000, transcendentals=0
        ),
    )(order, choice, *sources)


def add_terms_kernel(scale, start, order, choice, *rest):
    sources, terms, outs, (wide, sems) = rest[:2], rest[2], rest[3:-2], rest[-2:]
    fetch_wide(choice[1], sources, wide, sems)
    span = terms.shape[2]
    done = 0
    for upper_out, lower_out in zip(outs[0::2], outs[1::2]):
        for g in range(upper_out.shape[0]):
            upper, lower = block_pair(wide, order[start + done], span)
            at = 2 * done
            upper_out[g] = (upper * scale + terms[at].astype(jnp.float32)).astype(upper_out.dtype)
            lower_out[g] = (lower * scale + terms[at + 1].astype(jnp.float32)).astype(lower_out.dtype)
            done += 1


def add_terms(order, choice, sources, terms, start, counts, scale):
    dev_cols, rows = sources[0].shape
    span = rows // 2 + BLOCK
    shapes = [n for n in counts for half in (0, 1)]
    return pl.pallas_call(
        functools.partial(add_terms_kernel, scale, start),
        out_shape=[jax.ShapeDtypeStruct((n, BLOCK, span), jnp.bfloat16) for n in shapes],
        in_specs=[SMEM, SMEM] + [ANY] * len(sources) + [VMEM],
        out_specs=[VMEM] * len(shapes),
        scratch_shapes=[
            pltpu.VMEM((dev_cols, rows + rows // 2), jnp.bfloat16),
            pltpu.SemaphoreType.DMA((2,)),
        ],
        compiler_params=params(),
        cost_estimate=pl.CostEstimate(
            flops=4 * sum(counts) * BLOCK * span * dev_cols, bytes_accessed=10000000, transcendentals=0
        ),
    )(order, choice, *sources, terms)


def place_blocks(places, order, pieces, gram):
    count = gram.shape[0] // BLOCK
    for (place, half), piece in zip(places, pieces):
        span = piece.shape[2]
        for k in range(piece.shape[0]):
            index = 2 * order[place + k] + half
            top = pl.multiple_of(index * BLOCK, BLOCK)
            for shift in range(span // BLOCK):
                left = pl.multiple_of(((index + shift) % count) * BLOCK, BLOCK)
                block = piece[k, :, shift * BLOCK : (shift + 1) * BLOCK]
                gram[pl.ds(top, BLOCK), pl.ds(left, BLOCK)] = block
                if 0 < shift < span // BLOCK - 1:
                    gram[pl.ds(left, BLOCK), pl.ds(top, BLOCK)] = block.T


def unpack_kernel(places, order, *rest):
    place_blocks(places, order, rest[:-1], rest[-1])


def unpack(order, pieces, places, rows):
    return pl.pallas_call(
        functools.partial(unpack_kernel, places),
        out_shape=jax.ShapeDtypeStruct((rows, rows), jnp.bfloat16),
        in_specs=[SMEM] + [VMEM] * len(pieces),
        out_specs=VMEM,
        compiler_params=params(),
        cost_estimate=pl.CostEstimate(flops=0, bytes_accessed=20000000, transcendentals=0),
    )(order, *pieces)


LAST_PLACES = ((0, 0), (1, 0), (0, 1), (1, 1))


def step_kernel(which, order, choice, *rest):
    sources, gram_in, lasts = rest[:-13], rest[-13], rest[-12:-8]
    result, gram, columns, low, linear, ready, sems, out_sems = rest[-8:]
    rows = gram.shape[0]
    load = pltpu.make_async_copy(gram_in, gram, sems.at[0])
    load.start()
    fetching = fetches(choice[which], sources, columns, sems.at[pl.ds(1, 2)])
    load.wait()
    place_blocks(LAST_PLACES, order, lasts, gram)
    finish_fetches(fetching)

    def multiply(t, carry):
        at = pl.ds(pl.multiple_of(t * TILE, TILE), TILE)
        value = jnp.dot(columns[...], gram[:, at], preferred_element_type=jnp.float32)
        low[:, at] = value.astype(jnp.bfloat16)
        linear[:, at] = COEF_A * columns[:, at].astype(jnp.float32) + COEF_B * value
        return carry

    lax.fori_loop(0, rows // TILE, multiply, 0)
    leaving = []
    for n, (first, width) in enumerate(OUT_TILES):
        at = slice(first, first + width)
        value = jnp.dot(low[...], gram[:, at], preferred_element_type=jnp.float32)
        ready[:, at] = (linear[:, at] + COEF_C * value).astype(jnp.bfloat16)
        leaving.append(pltpu.make_async_copy(ready.at[:, at], result.at[:, at], out_sems.at[n]))
        leaving[-1].start()
    for copy in leaving:
        copy.wait()


def newton_step(which, order, choice, sources, gram, lasts):
    dev_cols, rows = sources[0].shape
    return pl.pallas_call(
        functools.partial(step_kernel, which),
        out_shape=jax.ShapeDtypeStruct((dev_cols, rows), jnp.bfloat16),
        in_specs=[SMEM, SMEM] + [ANY] * (len(sources) + 1) + [VMEM] * len(lasts),
        out_specs=ANY,
        scratch_shapes=[
            pltpu.VMEM((rows, rows), jnp.bfloat16),
            pltpu.VMEM((dev_cols, rows), jnp.bfloat16),
            pltpu.VMEM((dev_cols, rows), jnp.bfloat16),
            pltpu.VMEM((dev_cols, rows), jnp.float32),
            pltpu.VMEM((dev_cols, rows), jnp.bfloat16),
            pltpu.SemaphoreType.DMA((3,)),
            pltpu.SemaphoreType.DMA((len(OUT_TILES),)),
        ],
        compiler_params=params(),
        cost_estimate=pl.CostEstimate(
            flops=4 * rows * rows * dev_cols, bytes_accessed=12000000, transcendentals=0
        ),
    )(order, choice, *sources, gram, *lasts)


def token_kernel(gate_back, up_back, token):
    token[0] = 0


def after(*arrays):
    return pl.pallas_call(
        token_kernel,
        out_shape=jax.ShapeDtypeStruct((1,), jnp.int32),
        in_specs=[ANY] * len(arrays),
        out_specs=SMEM,
        compiler_params=pltpu.CompilerParams(vmem_limit_bytes=1024 * 1024),
    )(*arrays)


def finish_kernel(pick, token, own, over, gate_back, up_back, gate_out, up_out, staged, sems):
    kept = []
    for n, (back, out) in enumerate(((gate_back, gate_out), (up_back, up_out))):
        came = pltpu.make_async_copy(back, out, sems.at[n])
        pl.when(pick[n] == 2)(came.start)
        for k, source in enumerate((own, over)):
            stage = pltpu.make_async_copy(source, staged.at[n], sems.at[2 + n])
            pl.when(pick[n] == k)(stage.start)
            kept.append((pick[n] == k, stage, pltpu.make_async_copy(staged.at[n], out, sems.at[n])))
    for wanted, stage, leave in kept:

        @pl.when(wanted)
        def _(stage=stage, leave=leave):
            stage.wait()
            leave.start()

    for n, (back, out) in enumerate(((gate_back, gate_out), (up_back, up_out))):
        pltpu.make_async_copy(back, out, sems.at[n]).wait()


def finish(pick, own, over, gate_back, up_back):
    shape = jax.ShapeDtypeStruct(own.shape, own.dtype)
    return pl.pallas_call(
        finish_kernel,
        out_shape=[shape, shape],
        in_specs=[SMEM, SMEM, ANY, ANY, VMEM, VMEM],
        out_specs=[ANY, ANY],
        scratch_shapes=[pltpu.VMEM((2,) + own.shape, own.dtype), pltpu.SemaphoreType.DMA((4,))],
        compiler_params=pltpu.CompilerParams(vmem_limit_bytes=8 * 1024 * 1024),
    )(pick, after(gate_back, up_back), own, over, gate_back, up_back)


def add(*terms):
    return sum(t.astype(jnp.float32) for t in terms).astype(jnp.bfloat16)


def per_device(gate_grad, up_grad):
    rows, dev_cols = gate_grad.shape
    scale = 1.0 / (dev_cols * lax.axis_size(("row", "col")))
    gate, up = gate_grad.T, up_grad.T
    on_up = lax.axis_index("section") % 2
    y = lax.axis_index("row")
    z = lax.axis_index("col")
    y_low, y_high = ((y == 1) | (y == 2)).astype(jnp.int32), (y >= 2).astype(jnp.int32)
    z_low, z_high = ((z == 1) | (z == 2)).astype(jnp.int32), (z >= 2).astype(jnp.int32)
    on_gate = on_up == 0
    p = jnp.where(on_gate, z_low, y_low)
    q = jnp.where(on_gate, z_high, y_high)
    gate_part, up_part = y_low, z_low
    order = jnp.stack(
        [
            4 * stream + 2 * (p ^ dp) + (q ^ dq)
            for dp, dq in ((1, 1), (1, 0), (0, 1), (0, 0))
            for stream in (0, 1)
        ]
    )
    own_choice = jnp.where(on_gate, 2 * gate_part, 2 - up_part)
    choice = jnp.stack([own_choice, on_up])

    gate_in = send(gate, GATE_OUT)
    up_in = send(up, UP_OUT)
    over = send(jnp.where(on_gate, up, gate), OVER)
    own = (gate, up, over)
    partner = (gate_in, up_in)
    corner_terms, other_terms = own_terms(order, choice, own, scale)

    corner = add_terms(order, choice, partner, corner_terms, 0, (1, 1), scale)
    got_a = [send(corner[half], HOP_1) for half in (0, 1)]
    got_b = [send(corner[2 + half], HOP_2) for half in (0, 1)]
    rest = add_terms(order, choice, partner, other_terms, 2, (2, 2, 2), scale)
    totals, ones, twos, lasts, places = [], [], [], [], []
    for half in (0, 1):
        side_1, side_2, mine = rest[half], rest[2 + half], rest[4 + half]
        got_1 = send(side_1.at[1:2].set(add(side_1[1:2], got_b[half])), HOP_1)
        got_2 = send(side_2.at[0:1].set(add(side_2[0:1], got_a[half])), HOP_2)
        mine = add(mine, got_1, got_2)
        totals.append(add(mine, send(mine, HOP_3)))

    for half in (0, 1):
        ones.append(send(totals[half], HOP_1))
        twos.append(send(totals[half], HOP_2))
    for half in (0, 1):
        lasts.append(send(twos[half][0:1], HOP_1))
        lasts.append(send(ones[half][1:2], HOP_2))
    gram = unpack(
        order,
        ones + twos + totals,
        ((2, 0), (2, 1), (4, 0), (4, 1), (6, 0), (6, 1)),
        rows,
    )

    partner_next = newton_step(1, order, choice, partner, gram, lasts)
    gate_back = send(partner_next, reverse(GATE_OUT))
    up_back = send(partner_next, reverse(UP_OUT))
    lasts[0], partner_next = lax.optimization_barrier((lasts[0], partner_next))
    own_next = newton_step(0, order, choice, own, gram, lasts)
    over_back = send(own_next, reverse(OVER))

    pick = jnp.stack(
        [
            jnp.where(gate_part == on_up, on_up, 2),
            jnp.where(up_part == on_up, 1 - on_up, 2),
        ]
    )
    gate_next, up_next = finish(pick, own_next, over_back, gate_back, up_back)
    return gate_next.T, up_next.T


def solution(mesh):
    placed = (P("section", ("row", "col")), P("section", ("row", "col")))
    return jax.shard_map(
        per_device,
        mesh=mesh,
        in_specs=placed,
        out_specs=placed,
        check_vma=False,
    )
```

```python
import functools

import jax
import jax.numpy as jnp
from jax import lax
from jax.experimental import pallas as pl
from jax.experimental.pallas import tpu as pltpu
from jax.sharding import PartitionSpec as P

COEF_A = 3.4445
COEF_B = -4.775
COEF_C = 2.0315

AXES = ("section", "row", "col")
BLOCK = 128
PAIR = 2 * BLOCK
TILE = 1024
OUT_TILES = ((0, 1024), (1024, 512), (1536, 512))
ROW_CHUNKS = ((0, 96), (96, 96), (192, 80), (272, 80))
VMEM_LIMIT = 28 * 1024 * 1024
ANY = pl.BlockSpec(memory_space=pl.ANY)
SMEM = pl.BlockSpec(memory_space=pltpu.SMEM)
VMEM = pl.BlockSpec(memory_space=pltpu.VMEM)


def device_pairs(route):
    pairs = []
    for x in range(4):
        for core in range(2):
            for y in range(4):
                for z in range(4):
                    target = route(core, y, z)
                    if target is not None:
                        to_core, to_y, to_z = target
                        pairs.append(
                            (((x * 2 + core) * 4 + y) * 4 + z, ((x * 2 + to_core) * 4 + to_y) * 4 + to_z)
                        )
    return pairs


def outer(i):
    return i in (0, 3)


GATE_OUT = device_pairs(lambda c, y, z: (0, y ^ 1, z) if c == (1 if outer(y) else 0) else None)
UP_OUT = device_pairs(lambda c, y, z: (1, y, z ^ 1) if c == (1 if outer(z) else 0) else None)
OVER = device_pairs(lambda c, y, z: (1 - c, y, z) if (outer(z) if c == 0 else not outer(y)) else None)


def reverse(pairs):
    return [(b, a) for a, b in pairs]


HOP_1 = device_pairs(lambda c, y, z: (c, y, z ^ 1) if c == 0 else (c, y ^ 1, z))
HOP_2 = device_pairs(lambda c, y, z: (c, y, 3 - z) if c == 0 else (c, 3 - y, z))
HOP_3 = device_pairs(lambda c, y, z: (c, 3 - y, z) if c == 0 else (c, y, 3 - z))


def send(values, pairs):
    return lax.ppermute(values, AXES, pairs)


def params():
    return pltpu.CompilerParams(vmem_limit_bytes=VMEM_LIMIT)


def fetches(chosen, sources, columns, sems):
    copies = []
    for k, parts in enumerate((sources[0:1], sources[1:2], sources[2:])):
        first = 0
        for n, part in enumerate(parts):
            at = slice(first, first + part.shape[0])
            first += part.shape[0]
            copies.append((chosen == k, pltpu.make_async_copy(part, columns.at[at, :], sems.at[n])))
    for wanted, copy in copies:
        pl.when(wanted)(copy.start)
    return copies


def finish_fetches(copies):
    for wanted, copy in copies:
        pl.when(wanted)(copy.wait)


def fetch_wide(chosen, sources, wide, sems):
    rows = sources[0].shape[1]
    finish_fetches(fetches(chosen, sources, wide.at[:, 0:rows], sems))
    wide[:, rows : rows + rows // 2] = wide[:, 0 : rows // 2]


def block_pair(wide, index, span):
    first = pl.multiple_of(index * PAIR, PAIR)
    value = lax.dot_general(
        wide[:, pl.ds(first, PAIR)],
        wide[:, pl.ds(first, span + BLOCK)],
        (((0,), (0,)), ((), ())),
        preferred_element_type=jnp.float32,
    )
    return value[0:BLOCK, 0:span], value[BLOCK:PAIR, BLOCK : span + BLOCK]


def own_terms_kernel(scale, order, choice, *rest):
    sources, (corner, others, wide, sems) = rest[:-4], rest[-4:]
    fetch_wide(choice[0], sources, wide, sems)
    span = corner.shape[2]
    for out, start, pairs in ((corner, 0, 2), (others, 2, 6)):

        def one(g, carry, out=out, start=start):
            upper, lower = block_pair(wide, order[start + g], span)
            out[2 * g] = (upper * scale).astype(out.dtype)
            out[2 * g + 1] = (lower * scale).astype(out.dtype)
            return carry

        lax.fori_loop(0, pairs, one, 0)


def own_terms(order, choice, sources, scale):
    dev_cols, rows = sources[0].shape
    span = rows // 2 + BLOCK
    return pl.pallas_call(
        functools.partial(own_terms_kernel, scale),
        out_shape=[jax.ShapeDtypeStruct((n, BLOCK, span), jnp.bfloat16) for n in (4, 12)],
        in_specs=[SMEM, SMEM] + [ANY] * len(sources),
        out_specs=[VMEM, VMEM],
        scratch_shapes=[
            pltpu.VMEM((dev_cols, rows + rows // 2), jnp.bfloat16),
            pltpu.SemaphoreType.DMA((2,)),
        ],
        compiler_params=params(),
        cost_estimate=pl.CostEstimate(
            flops=0, bytes_accessed=1000, transcendentals=0
        ),
    )(order, choice, *sources)


def add_terms_kernel(scale, start, order, choice, *rest):
    sources, terms, outs, (wide, sems) = rest[:2], rest[2], rest[3:-2], rest[-2:]
    fetch_wide(choice[1], sources, wide, sems)
    span = terms.shape[2]
    done = 0
    for upper_out, lower_out in zip(outs[0::2], outs[1::2]):
        for g in range(upper_out.shape[0]):
            upper, lower = block_pair(wide, order[start + done], span)
            at = 2 * done
            upper_out[g] = (upper * scale + terms[at].astype(jnp.float32)).astype(upper_out.dtype)
            lower_out[g] = (lower * scale + terms[at + 1].astype(jnp.float32)).astype(lower_out.dtype)
            done += 1


def add_terms(order, choice, sources, terms, start, counts, scale):
    dev_cols, rows = sources[0].shape
    span = rows // 2 + BLOCK
    shapes = [n for n in counts for half in (0, 1)]
    return pl.pallas_call(
        functools.partial(add_terms_kernel, scale, start),
        out_shape=[jax.ShapeDtypeStruct((n, BLOCK, span), jnp.bfloat16) for n in shapes],
        in_specs=[SMEM, SMEM] + [ANY] * len(sources) + [VMEM],
        out_specs=[VMEM] * len(shapes),
        scratch_shapes=[
            pltpu.VMEM((dev_cols, rows + rows // 2), jnp.bfloat16),
            pltpu.SemaphoreType.DMA((2,)),
        ],
        compiler_params=params(),
        cost_estimate=pl.CostEstimate(
            flops=4 * sum(counts) * BLOCK * span * dev_cols, bytes_accessed=10000000, transcendentals=0
        ),
    )(order, choice, *sources, terms)


def place_blocks(places, order, pieces, gram):
    count = gram.shape[0] // BLOCK
    for (place, half), piece in zip(places, pieces):
        span = piece.shape[2]
        for k in range(piece.shape[0]):
            index = 2 * order[place + k] + half
            top = pl.multiple_of(index * BLOCK, BLOCK)
            for shift in range(span // BLOCK):
                left = pl.multiple_of(((index + shift) % count) * BLOCK, BLOCK)
                block = piece[k, :, shift * BLOCK : (shift + 1) * BLOCK]
                gram[pl.ds(top, BLOCK), pl.ds(left, BLOCK)] = block
                if 0 < shift < span // BLOCK - 1:
                    gram[pl.ds(left, BLOCK), pl.ds(top, BLOCK)] = block.T


def unpack_kernel(places, order, *rest):
    place_blocks(places, order, rest[:-1], rest[-1])


def unpack(order, pieces, places, rows):
    return pl.pallas_call(
        functools.partial(unpack_kernel, places),
        out_shape=jax.ShapeDtypeStruct((rows, rows), jnp.bfloat16),
        in_specs=[SMEM] + [VMEM] * len(pieces),
        out_specs=VMEM,
        compiler_params=params(),
        cost_estimate=pl.CostEstimate(flops=0, bytes_accessed=20000000, transcendentals=0),
    )(order, *pieces)


LAST_PLACES = ((0, 0), (1, 0), (0, 1), (1, 1))


def step_kernel(which, order, choice, *rest):
    sources, gram_in, lasts = rest[:-13], rest[-13], rest[-12:-8]
    result, gram, columns, low, linear, ready, sems, out_sems = rest[-8:]
    rows = gram.shape[0]
    load = pltpu.make_async_copy(gram_in, gram, sems.at[0])
    load.start()
    fetching = fetches(choice[which], sources, columns, sems.at[pl.ds(1, 2)])
    load.wait()
    place_blocks(LAST_PLACES, order, lasts, gram)
    finish_fetches(fetching)

    def multiply(t, carry):
        at = pl.ds(pl.multiple_of(t * TILE, TILE), TILE)
        value = jnp.dot(columns[...], gram[:, at], preferred_element_type=jnp.float32)
        low[:, at] = value.astype(jnp.bfloat16)
        linear[:, at] = COEF_A * columns[:, at].astype(jnp.float32) + COEF_B * value
        return carry

    lax.fori_loop(0, rows // TILE, multiply, 0)
    leaving = []
    for n, (first, width) in enumerate(OUT_TILES):
        at = slice(first, first + width)
        value = jnp.dot(low[...], gram[:, at], preferred_element_type=jnp.float32)
        ready[:, at] = (linear[:, at] + COEF_C * value).astype(jnp.bfloat16)
        leaving.append(pltpu.make_async_copy(ready.at[:, at], result.at[:, at], out_sems.at[n]))
        leaving[-1].start()
    for copy in leaving:
        copy.wait()


def newton_step(which, order, choice, sources, gram, lasts):
    dev_cols, rows = sources[0].shape
    return pl.pallas_call(
        functools.partial(step_kernel, which),
        out_shape=jax.ShapeDtypeStruct((dev_cols, rows), jnp.bfloat16),
        in_specs=[SMEM, SMEM] + [ANY] * (len(sources) + 1) + [VMEM] * len(lasts),
        out_specs=ANY,
        scratch_shapes=[
            pltpu.VMEM((rows, rows), jnp.bfloat16),
            pltpu.VMEM((dev_cols, rows), jnp.bfloat16),
            pltpu.VMEM((dev_cols, rows), jnp.bfloat16),
            pltpu.VMEM((dev_cols, rows), jnp.float32),
            pltpu.VMEM((dev_cols, rows), jnp.bfloat16),
            pltpu.SemaphoreType.DMA((3,)),
            pltpu.SemaphoreType.DMA((len(OUT_TILES),)),
        ],
        compiler_params=params(),
        cost_estimate=pl.CostEstimate(
            flops=4 * rows * rows * dev_cols, bytes_accessed=12000000, transcendentals=0
        ),
    )(order, choice, *sources, gram, *lasts)


def token_kernel(gate_back, up_back, token):
    token[0] = 0


def after(*arrays):
    return pl.pallas_call(
        token_kernel,
        out_shape=jax.ShapeDtypeStruct((1,), jnp.int32),
        in_specs=[ANY] * len(arrays),
        out_specs=SMEM,
        compiler_params=pltpu.CompilerParams(vmem_limit_bytes=1024 * 1024),
    )(*arrays)


def finish_kernel(pick, token, own, over, gate_back, up_back, gate_out, up_out, staged, in_sems, out_sems):
    arrivals, departures = [], []
    for c, (first, count) in enumerate(ROW_CHUNKS):
        at = slice(first, first + count)
        for n, (back, out) in enumerate(((gate_back, gate_out), (up_back, up_out))):
            for k, source in enumerate((own, over, back)):
                arrivals.append(
                    (
                        pick[n] == k,
                        pltpu.make_async_copy(source.at[at, :], staged.at[n, at, :], in_sems.at[n, c]),
                    )
                )
            departures.append(pltpu.make_async_copy(staged.at[n, at, :], out.at[at, :], out_sems.at[n, c]))
    for wanted, copy in arrivals:
        pl.when(wanted)(copy.start)
    for d, copy in enumerate(departures):
        for wanted, arrival in arrivals[3 * d : 3 * d + 3]:
            pl.when(wanted)(arrival.wait)
        copy.start()
    for copy in departures:
        copy.wait()


def finish(pick, own, over, gate_back, up_back):
    shape = jax.ShapeDtypeStruct(own.shape, own.dtype)
    return pl.pallas_call(
        finish_kernel,
        out_shape=[shape, shape],
        in_specs=[SMEM, SMEM] + [ANY] * 4,
        out_specs=[ANY, ANY],
        scratch_shapes=[
            pltpu.VMEM((2,) + own.shape, own.dtype),
            pltpu.SemaphoreType.DMA((2, len(ROW_CHUNKS))),
            pltpu.SemaphoreType.DMA((2, len(ROW_CHUNKS))),
        ],
        compiler_params=pltpu.CompilerParams(vmem_limit_bytes=8 * 1024 * 1024),
    )(pick, after(gate_back, up_back), own, over, gate_back, up_back)


def add(*terms):
    return sum(t.astype(jnp.float32) for t in terms).astype(jnp.bfloat16)


def per_device(gate_grad, up_grad):
    rows, dev_cols = gate_grad.shape
    scale = 1.0 / (dev_cols * lax.axis_size(("row", "col")))
    gate, up = gate_grad.T, up_grad.T
    on_up = lax.axis_index("section") % 2
    y = lax.axis_index("row")
    z = lax.axis_index("col")
    y_low, y_high = ((y == 1) | (y == 2)).astype(jnp.int32), (y >= 2).astype(jnp.int32)
    z_low, z_high = ((z == 1) | (z == 2)).astype(jnp.int32), (z >= 2).astype(jnp.int32)
    on_gate = on_up == 0
    p = jnp.where(on_gate, z_low, y_low)
    q = jnp.where(on_gate, z_high, y_high)
    gate_part, up_part = y_low, z_low
    order = jnp.stack(
        [
            4 * stream + 2 * (p ^ dp) + (q ^ dq)
            for dp, dq in ((1, 1), (1, 0), (0, 1), (0, 0))
            for stream in (0, 1)
        ]
    )
    own_choice = jnp.where(on_gate, 2 * gate_part, 2 - up_part)
    choice = jnp.stack([own_choice, on_up])

    gate_in = send(gate, GATE_OUT)
    up_in = send(up, UP_OUT)
    over = jnp.where(on_gate, up, gate)
    own = (gate, up, send(over[: dev_cols // 2], OVER), send(over[dev_cols // 2 :], OVER))
    partner = (gate_in, up_in)
    corner_terms, other_terms = own_terms(order, choice, own, scale)

    corner = add_terms(order, choice, partner, corner_terms, 0, (1, 1), scale)
    got_a = [send(corner[half], HOP_1) for half in (0, 1)]
    got_b = [send(corner[2 + half], HOP_2) for half in (0, 1)]
    rest = add_terms(order, choice, partner, other_terms, 2, (2, 2, 2), scale)
    totals, ones, twos, lasts, places = [], [], [], [], []
    for half in (0, 1):
        side_1, side_2, mine = rest[half], rest[2 + half], rest[4 + half]
        got_1 = send(side_1.at[1:2].set(add(side_1[1:2], got_b[half])), HOP_1)
        got_2 = send(side_2.at[0:1].set(add(side_2[0:1], got_a[half])), HOP_2)
        mine = add(mine, got_1, got_2)
        totals.append(add(mine, send(mine, HOP_3)))

    for half in (0, 1):
        ones.append(send(totals[half], HOP_1))
        twos.append(send(totals[half], HOP_2))
    for half in (0, 1):
        lasts.append(send(twos[half][0:1], HOP_1))
        lasts.append(send(ones[half][1:2], HOP_2))
    gram = unpack(
        order,
        ones + twos + totals,
        ((2, 0), (2, 1), (4, 0), (4, 1), (6, 0), (6, 1)),
        rows,
    )

    partner_next = newton_step(1, order, choice, partner, gram, lasts)
    gate_back = send(partner_next, reverse(GATE_OUT))
    up_back = send(partner_next, reverse(UP_OUT))
    lasts[0], partner_next = lax.optimization_barrier((lasts[0], partner_next))
    own_next = newton_step(0, order, choice, own, gram, lasts)
    over_back = send(own_next, reverse(OVER))

    pick = jnp.stack(
        [
            jnp.where(gate_part == on_up, on_up, 2),
            jnp.where(up_part == on_up, 1 - on_up, 2),
        ]
    )
    gate_next, up_next = finish(pick, own_next, over_back, gate_back, up_back)
    return gate_next.T, up_next.T


def solution(mesh):
    placed = (P("section", ("row", "col")), P("section", ("row", "col")))
    return jax.shard_map(
        per_device,
        mesh=mesh,
        in_specs=placed,
        out_specs=placed,
        check_vma=False,
    )
```

```python
import functools

import jax
import jax.numpy as jnp
from jax import lax
from jax.experimental import pallas as pl
from jax.experimental.pallas import tpu as pltpu
from jax.sharding import PartitionSpec as P

COEF_A = 3.4445
COEF_B = -4.775
COEF_C = 2.0315

AXES = ("section", "row", "col")
BLOCK = 128
PAIR = 2 * BLOCK
TILE = 2048
OUT_TILES = ((0, 1024), (1024, 768), (1792, 256))
ROW_CHUNKS = ((0, 96), (96, 96), (192, 80), (272, 80))
VMEM_LIMIT = 28 * 1024 * 1024
ANY = pl.BlockSpec(memory_space=pl.ANY)
SMEM = pl.BlockSpec(memory_space=pltpu.SMEM)
VMEM = pl.BlockSpec(memory_space=pltpu.VMEM)


def device_pairs(route):
    pairs = []
    for x in range(4):
        for core in range(2):
            for y in range(4):
                for z in range(4):
                    target = route(core, y, z)
                    if target is not None:
                        to_core, to_y, to_z = target
                        pairs.append(
                            (((x * 2 + core) * 4 + y) * 4 + z, ((x * 2 + to_core) * 4 + to_y) * 4 + to_z)
                        )
    return pairs


def outer(i):
    return i in (0, 3)


GATE_OUT = device_pairs(lambda c, y, z: (0, y ^ 1, z) if c == (1 if outer(y) else 0) else None)
UP_OUT = device_pairs(lambda c, y, z: (1, y, z ^ 1) if c == (1 if outer(z) else 0) else None)
OVER = device_pairs(lambda c, y, z: (1 - c, y, z) if (outer(z) if c == 0 else not outer(y)) else None)


def reverse(pairs):
    return [(b, a) for a, b in pairs]


HOP_1 = device_pairs(lambda c, y, z: (c, y, z ^ 1) if c == 0 else (c, y ^ 1, z))
HOP_2 = device_pairs(lambda c, y, z: (c, y, 3 - z) if c == 0 else (c, 3 - y, z))
HOP_3 = device_pairs(lambda c, y, z: (c, 3 - y, z) if c == 0 else (c, y, 3 - z))


def send(values, pairs):
    return lax.ppermute(values, AXES, pairs)


def params():
    return pltpu.CompilerParams(vmem_limit_bytes=VMEM_LIMIT)


def fetches(chosen, sources, columns, sems):
    copies = []
    for k, parts in enumerate((sources[0:1], sources[1:2], sources[2:])):
        first = 0
        for n, part in enumerate(parts):
            at = slice(first, first + part.shape[0])
            first += part.shape[0]
            copies.append((chosen == k, pltpu.make_async_copy(part, columns.at[at, :], sems.at[n])))
    for wanted, copy in copies:
        pl.when(wanted)(copy.start)
    return copies


def finish_fetches(copies):
    for wanted, copy in copies:
        pl.when(wanted)(copy.wait)


def fetch_wide(chosen, sources, wide, sems):
    rows = sources[0].shape[1]
    finish_fetches(fetches(chosen, sources, wide.at[:, 0:rows], sems))
    wide[:, rows : rows + rows // 2] = wide[:, 0 : rows // 2]


def block_pair(wide, index, span):
    first = pl.multiple_of(index * PAIR, PAIR)
    value = lax.dot_general(
        wide[:, pl.ds(first, PAIR)],
        wide[:, pl.ds(first, span + BLOCK)],
        (((0,), (0,)), ((), ())),
        preferred_element_type=jnp.float32,
    )
    return value[0:BLOCK, 0:span], value[BLOCK:PAIR, BLOCK : span + BLOCK]


def own_terms_kernel(scale, order, choice, *rest):
    sources, (corner, others, wide, sems) = rest[:-4], rest[-4:]
    fetch_wide(choice[0], sources, wide, sems)
    span = corner.shape[2]
    for out, start, pairs in ((corner, 0, 2), (others, 2, 6)):

        def one(g, carry, out=out, start=start):
            upper, lower = block_pair(wide, order[start + g], span)
            out[2 * g] = (upper * scale).astype(out.dtype)
            out[2 * g + 1] = (lower * scale).astype(out.dtype)
            return carry

        lax.fori_loop(0, pairs, one, 0)


def own_terms(order, choice, sources, scale):
    dev_cols, rows = sources[0].shape
    span = rows // 2 + BLOCK
    return pl.pallas_call(
        functools.partial(own_terms_kernel, scale),
        out_shape=[jax.ShapeDtypeStruct((n, BLOCK, span), jnp.bfloat16) for n in (4, 12)],
        in_specs=[SMEM, SMEM] + [ANY] * len(sources),
        out_specs=[VMEM, VMEM],
        scratch_shapes=[
            pltpu.VMEM((dev_cols, rows + rows // 2), jnp.bfloat16),
            pltpu.SemaphoreType.DMA((2,)),
        ],
        compiler_params=params(),
        cost_estimate=pl.CostEstimate(
            flops=0, bytes_accessed=1000, transcendentals=0
        ),
    )(order, choice, *sources)


def add_terms_kernel(scale, start, order, choice, *rest):
    sources, terms, outs, (wide, sems) = rest[:2], rest[2], rest[3:-2], rest[-2:]
    fetch_wide(choice[1], sources, wide, sems)
    span = terms.shape[2]
    done = 0
    for upper_out, lower_out in zip(outs[0::2], outs[1::2]):
        for g in range(upper_out.shape[0]):
            upper, lower = block_pair(wide, order[start + done], span)
            at = 2 * done
            upper_out[g] = (upper * scale + terms[at].astype(jnp.float32)).astype(upper_out.dtype)
            lower_out[g] = (lower * scale + terms[at + 1].astype(jnp.float32)).astype(lower_out.dtype)
            done += 1


def add_terms(order, choice, sources, terms, start, counts, scale):
    dev_cols, rows = sources[0].shape
    span = rows // 2 + BLOCK
    shapes = [n for n in counts for half in (0, 1)]
    return pl.pallas_call(
        functools.partial(add_terms_kernel, scale, start),
        out_shape=[jax.ShapeDtypeStruct((n, BLOCK, span), jnp.bfloat16) for n in shapes],
        in_specs=[SMEM, SMEM] + [ANY] * len(sources) + [VMEM],
        out_specs=[VMEM] * len(shapes),
        scratch_shapes=[
            pltpu.VMEM((dev_cols, rows + rows // 2), jnp.bfloat16),
            pltpu.SemaphoreType.DMA((2,)),
        ],
        compiler_params=params(),
        cost_estimate=pl.CostEstimate(
            flops=4 * sum(counts) * BLOCK * span * dev_cols, bytes_accessed=10000000, transcendentals=0
        ),
    )(order, choice, *sources, terms)


def place_blocks(places, order, pieces, gram):
    count = gram.shape[0] // BLOCK
    for (place, half), piece in zip(places, pieces):
        span = piece.shape[2]
        for k in range(piece.shape[0]):
            index = 2 * order[place + k] + half
            top = pl.multiple_of(index * BLOCK, BLOCK)
            for shift in range(span // BLOCK):
                left = pl.multiple_of(((index + shift) % count) * BLOCK, BLOCK)
                block = piece[k, :, shift * BLOCK : (shift + 1) * BLOCK]
                gram[pl.ds(top, BLOCK), pl.ds(left, BLOCK)] = block
                if 0 < shift < span // BLOCK - 1:
                    gram[pl.ds(left, BLOCK), pl.ds(top, BLOCK)] = block.T


def unpack_kernel(places, order, *rest):
    place_blocks(places, order, rest[:-1], rest[-1])


def unpack(order, pieces, places, rows):
    return pl.pallas_call(
        functools.partial(unpack_kernel, places),
        out_shape=jax.ShapeDtypeStruct((rows, rows), jnp.bfloat16),
        in_specs=[SMEM] + [VMEM] * len(pieces),
        out_specs=VMEM,
        compiler_params=params(),
        cost_estimate=pl.CostEstimate(flops=0, bytes_accessed=20000000, transcendentals=0),
    )(order, *pieces)


LAST_PLACES = ((0, 0), (1, 0), (0, 1), (1, 1))


def step_kernel(which, order, choice, *rest):
    sources, gram_in, lasts = rest[:-13], rest[-13], rest[-12:-8]
    result, gram, columns, low, linear, ready, sems, out_sems = rest[-8:]
    rows = gram.shape[0]
    load = pltpu.make_async_copy(gram_in, gram, sems.at[0])
    load.start()
    fetching = fetches(choice[which], sources, columns, sems.at[pl.ds(1, 2)])
    load.wait()
    place_blocks(LAST_PLACES, order, lasts, gram)
    finish_fetches(fetching)

    def multiply(t, carry):
        at = pl.ds(pl.multiple_of(t * TILE, TILE), TILE)
        value = jnp.dot(columns[...], gram[:, at], preferred_element_type=jnp.float32)
        low[:, at] = value.astype(jnp.bfloat16)
        linear[:, at] = COEF_A * columns[:, at].astype(jnp.float32) + COEF_B * value
        return carry

    lax.fori_loop(0, rows // TILE, multiply, 0)
    leaving = []
    for n, (first, width) in enumerate(OUT_TILES):
        at = slice(first, first + width)
        value = jnp.dot(low[...], gram[:, at], preferred_element_type=jnp.float32)
        ready[:, at] = (linear[:, at] + COEF_C * value).astype(jnp.bfloat16)
        leaving.append(pltpu.make_async_copy(ready.at[:, at], result.at[:, at], out_sems.at[n]))
        leaving[-1].start()
    for copy in leaving:
        copy.wait()


def newton_step(which, order, choice, sources, gram, lasts):
    dev_cols, rows = sources[0].shape
    return pl.pallas_call(
        functools.partial(step_kernel, which),
        out_shape=jax.ShapeDtypeStruct((dev_cols, rows), jnp.bfloat16),
        in_specs=[SMEM, SMEM] + [ANY] * (len(sources) + 1) + [VMEM] * len(lasts),
        out_specs=ANY,
        scratch_shapes=[
            pltpu.VMEM((rows, rows), jnp.bfloat16),
            pltpu.VMEM((dev_cols, rows), jnp.bfloat16),
            pltpu.VMEM((dev_cols, rows), jnp.bfloat16),
            pltpu.VMEM((dev_cols, rows), jnp.float32),
            pltpu.VMEM((dev_cols, rows), jnp.bfloat16),
            pltpu.SemaphoreType.DMA((3,)),
            pltpu.SemaphoreType.DMA((len(OUT_TILES),)),
        ],
        compiler_params=params(),
        cost_estimate=pl.CostEstimate(
            flops=4 * rows * rows * dev_cols, bytes_accessed=12000000, transcendentals=0
        ),
    )(order, choice, *sources, gram, *lasts)


def token_kernel(gate_back, up_back, token):
    token[0] = 0


def after(*arrays):
    return pl.pallas_call(
        token_kernel,
        out_shape=jax.ShapeDtypeStruct((1,), jnp.int32),
        in_specs=[ANY] * len(arrays),
        out_specs=SMEM,
        compiler_params=pltpu.CompilerParams(vmem_limit_bytes=1024 * 1024),
    )(*arrays)


def finish_kernel(pick, token, own, over, gate_back, up_back, gate_out, up_out, staged, in_sems, out_sems):
    arrivals, departures = [], []
    for c, (first, count) in enumerate(ROW_CHUNKS):
        at = slice(first, first + count)
        for n, (back, out) in enumerate(((gate_back, gate_out), (up_back, up_out))):
            for k, source in enumerate((own, over, back)):
                arrivals.append(
                    (
                        pick[n] == k,
                        pltpu.make_async_copy(source.at[at, :], staged.at[n, at, :], in_sems.at[n, c]),
                    )
                )
            departures.append(pltpu.make_async_copy(staged.at[n, at, :], out.at[at, :], out_sems.at[n, c]))
    for wanted, copy in arrivals:
        pl.when(wanted)(copy.start)
    for d, copy in enumerate(departures):
        for wanted, arrival in arrivals[3 * d : 3 * d + 3]:
            pl.when(wanted)(arrival.wait)
        copy.start()
    for copy in departures:
        copy.wait()


def finish(pick, own, over, gate_back, up_back):
    shape = jax.ShapeDtypeStruct(own.shape, own.dtype)
    return pl.pallas_call(
        finish_kernel,
        out_shape=[shape, shape],
        in_specs=[SMEM, SMEM] + [ANY] * 4,
        out_specs=[ANY, ANY],
        scratch_shapes=[
            pltpu.VMEM((2,) + own.shape, own.dtype),
            pltpu.SemaphoreType.DMA((2, len(ROW_CHUNKS))),
            pltpu.SemaphoreType.DMA((2, len(ROW_CHUNKS))),
        ],
        compiler_params=pltpu.CompilerParams(vmem_limit_bytes=8 * 1024 * 1024),
    )(pick, after(gate_back, up_back), own, over, gate_back, up_back)


def add(*terms):
    return sum(t.astype(jnp.float32) for t in terms).astype(jnp.bfloat16)


def per_device(gate_grad, up_grad):
    rows, dev_cols = gate_grad.shape
    scale = 1.0 / (dev_cols * lax.axis_size(("row", "col")))
    gate, up = gate_grad.T, up_grad.T
    on_up = lax.axis_index("section") % 2
    y = lax.axis_index("row")
    z = lax.axis_index("col")
    y_low, y_high = ((y == 1) | (y == 2)).astype(jnp.int32), (y >= 2).astype(jnp.int32)
    z_low, z_high = ((z == 1) | (z == 2)).astype(jnp.int32), (z >= 2).astype(jnp.int32)
    on_gate = on_up == 0
    p = jnp.where(on_gate, z_low, y_low)
    q = jnp.where(on_gate, z_high, y_high)
    gate_part, up_part = y_low, z_low
    order = jnp.stack(
        [
            4 * stream + 2 * (p ^ dp) + (q ^ dq)
            for dp, dq in ((1, 1), (1, 0), (0, 1), (0, 0))
            for stream in (0, 1)
        ]
    )
    own_choice = jnp.where(on_gate, 2 * gate_part, 2 - up_part)
    choice = jnp.stack([own_choice, on_up])

    gate_in = send(gate, GATE_OUT)
    up_in = send(up, UP_OUT)
    over = jnp.where(on_gate, up, gate)
    own = (gate, up, send(over[: dev_cols // 2], OVER), send(over[dev_cols // 2 :], OVER))
    partner = (gate_in, up_in)
    corner_terms, other_terms = own_terms(order, choice, own, scale)

    corner = add_terms(order, choice, partner, corner_terms, 0, (1, 1), scale)
    got_a = [send(corner[half], HOP_1) for half in (0, 1)]
    got_b = [send(corner[2 + half], HOP_2) for half in (0, 1)]
    rest = add_terms(order, choice, partner, other_terms, 2, (2, 2, 2), scale)
    totals, ones, twos, lasts, places = [], [], [], [], []
    for half in (0, 1):
        side_1, side_2, mine = rest[half], rest[2 + half], rest[4 + half]
        got_1 = send(side_1.at[1:2].set(add(side_1[1:2], got_b[half])), HOP_1)
        got_2 = send(side_2.at[0:1].set(add(side_2[0:1], got_a[half])), HOP_2)
        mine = add(mine, got_1, got_2)
        totals.append(add(mine, send(mine, HOP_3)))

    for half in (0, 1):
        ones.append(send(totals[half], HOP_1))
        twos.append(send(totals[half], HOP_2))
    for half in (0, 1):
        lasts.append(send(twos[half][0:1], HOP_1))
        lasts.append(send(ones[half][1:2], HOP_2))
    gram = unpack(
        order,
        ones + twos + totals,
        ((2, 0), (2, 1), (4, 0), (4, 1), (6, 0), (6, 1)),
        rows,
    )

    partner_next = newton_step(1, order, choice, partner, gram, lasts)
    gate_back = send(partner_next, reverse(GATE_OUT))
    up_back = send(partner_next, reverse(UP_OUT))
    lasts[0], partner_next = lax.optimization_barrier((lasts[0], partner_next))
    own_next = newton_step(0, order, choice, own, gram, lasts)
    over_back = send(own_next, reverse(OVER))

    pick = jnp.stack(
        [
            jnp.where(gate_part == on_up, on_up, 2),
            jnp.where(up_part == on_up, 1 - on_up, 2),
        ]
    )
    gate_next, up_next = finish(pick, own_next, over_back, gate_back, up_back)
    return gate_next.T, up_next.T


def solution(mesh):
    placed = (P("section", ("row", "col")), P("section", ("row", "col")))
    return jax.shard_map(
        per_device,
        mesh=mesh,
        in_specs=placed,
        out_specs=placed,
        check_vma=False,
    )
```
